32 devices in a mesh: rows: 16 (over z, x, core), dirs: 2 (over y).
Axes of the slice: x: 2, y: 2, z: 4, core: 2. Of those that a mesh axis runs over, the one named last changes fastest.
Arguments:
- previous: bfloat16 [24, 32, 128, 512], P('dirs', None, 'rows'), may hold values from -12 to 12
- boundary: float32 [24, 32, 512], P('dirs'), may hold values from -6 to 6
- row_coupling: float32 [24, 128, 512], P('dirs', 'rows'), may hold values from 0 to 1
- cross_gain: float32 [24], P('dirs'), may hold values from 0.5 to 3
- block_inverse: float32 [24, 128, 128], P('dirs'), may hold values from 0 to 1, as said below
- quadrant: int32 [24], P('dirs'), may hold values from 0 to 3
- sea_mask: int32 [128, 512], P('rows'), may hold values from 0 to 1, as said below
- wet_tiles: int32 [128, 4], P('rows'), may hold values 0 or 1
- quad_coef: float32 [32], replicated, may hold values from 0.05 to 0.5
Outputs:
- action: bfloat16 [24, 32, 128, 512], P('dirs', None, 'rows')
The draws below stay inside these ranges and needn't reach their ends.
Inputs may be any that keep to these rules, and one draw needn't show every extreme that they name: `sea_mask`: in each row the land cells, if any, are the last ones, from a coastline column to the end of the row. block_inverse[d] is the inverse of the 128 x 128 lower bidiagonal matrix with 1 + cross_gain[d] on its diagonal and -cross_gain[d] just below it.
All inputs are finite; a program needn't handle non-finite values. No bound on the sum of `wet_tiles` on one device may be relied on, other than what follows from the above.
Results may differ from the reference program's by a relative error of at most 0.0027.
Values may be sent and summed in bfloat16 or wider, within the bound.
A program may use at most 128 MiB of HBM per device.

```python
import math
import jax
import jax.numpy as jnp
from jax import lax

SPECTRAL_ANGLES = 24
FREQ = 32
BLOCK = 128
SHIFT = 2
CX = 8
NY = 512
GRID_ROW_TOTAL = 128


def coupling_gains(key):
    unit = jax.random.uniform(jax.random.fold_in(key, 11), (SPECTRAL_ANGLES,), jnp.float32)
    return jnp.exp(jnp.log(0.5) + unit * (jnp.log(3.0) - jnp.log(0.5)))


def draw_cross_gain(key, part):
    return coupling_gains(key)


def draw_block_inverse(key, part):
    gains = coupling_gains(key)
    ratio = gains / (1.0 + gains)
    lower = jnp.arange(BLOCK)[:, None]
    upper = jnp.arange(BLOCK)[None, :]
    offset = jnp.maximum(lower - upper, 0).astype(jnp.float32)
    power = jnp.exp(offset[None] * jnp.log(ratio)[:, None, None])
    return jnp.where((lower >= upper)[None], power / (1.0 + gains)[:, None, None], 0.0).astype(jnp.float32)


def draw_sea_mask(key, part):
    stretch_count = 4
    coast_widths = jax.random.randint(jax.random.fold_in(key, 21), (stretch_count,), 1, NY // 2)
    ranking = jax.random.permutation(jax.random.fold_in(key, 22), stretch_count)
    coast_widths = jnp.where(ranking < 2, 0, coast_widths)
    stretch_of_row = jnp.arange(GRID_ROW_TOTAL) * stretch_count // GRID_ROW_TOTAL
    matching = stretch_of_row[:, None] == jnp.arange(stretch_count)[None, :]
    row_widths = jnp.sum(jnp.where(matching, coast_widths[None, :], 0), axis=1)
    column = jnp.arange(NY)[None, :]
    return (column < NY - row_widths[:, None]).astype(jnp.int32)


def draw_row_coupling(key, part):
    random_keys = jax.random.split(jax.random.fold_in(key, 31), 6)
    slow_pick = jax.random.bernoulli(random_keys[0], 0.5, (SPECTRAL_ANGLES,))
    slow_unit = jax.random.uniform(random_keys[1], (SPECTRAL_ANGLES,), jnp.float32)
    slow_rate = jnp.exp(jnp.log(0.1 / GRID_ROW_TOTAL) + slow_unit * (jnp.log(0.6 / GRID_ROW_TOTAL) - jnp.log(0.1 / GRID_ROW_TOTAL)))
    fast_unit = jax.random.uniform(random_keys[2], (SPECTRAL_ANGLES,), jnp.float32)
    fast_rate = jnp.exp(jnp.log(1.0 / 50.0) + fast_unit * (jnp.log(1.0 / 30.0) - jnp.log(1.0 / 50.0)))
    rates = jnp.where(slow_pick, slow_rate, fast_rate)
    spread = jax.random.uniform(random_keys[3], (SPECTRAL_ANGLES, GRID_ROW_TOTAL, NY), jnp.float32, 0.5, 2.0)
    gusty_rows = jax.random.randint(random_keys[4], (SPECTRAL_ANGLES, 2), 0, GRID_ROW_TOTAL)
    impacted_cells = jnp.any(jnp.arange(GRID_ROW_TOTAL)[None, None, :] == gusty_rows[:, :, None], axis=1)
    depth = jax.random.uniform(random_keys[5], (SPECTRAL_ANGLES, GRID_ROW_TOTAL), jnp.float32, 0.6, 0.85)
    factor = jnp.where(impacted_cells, depth, 1.0)
    return (jnp.exp(-rates[:, None, None] * spread) * factor[:, :, None]).astype(jnp.float32)


def set_ends(array, key, low, top_value):
    longest = array.shape.index(max(array.shape))
    spots = []
    for shift in (0, 1):
        where = [jax.random.randint(jax.random.fold_in(key, axis), (), 0, length) for axis, length in enumerate(array.shape)]
        where[longest] = (where[longest] + shift) % array.shape[longest]
        spots.append(tuple(where))
    return array.at[spots[0]].set(low).at[spots[1]].set(top_value)


def block_scale(rng, dims, shards, least, high):
    level, own = 1.0, jax.random.fold_in(rng, 6)
    for axis_at, shards_of in shards:
        steps = jnp.exp(jax.random.uniform(jax.random.fold_in(own, axis_at), (shards_of,), jnp.float32, least / len(shards), high / len(shards)))
        level = level * jnp.repeat(steps, dims[axis_at] // shards_of).reshape([-1 if axis == axis_at else 1 for axis in range(len(dims))])
    return level


def centred(stream_key, shape, scale, reach, shards=(), dtype=jnp.bfloat16):
    entries = jax.random.normal(stream_key, shape, jnp.float32) * scale
    if len(shards) > 0:
        entries = block_scale(stream_key, shape, shards, -0.22, 0.18) * entries
    return jnp.clip(entries, min=-reach, max=reach).astype(dtype)


def setup_inputs(seed: int = 0) -> dict:
    key_list = jax.random.split(jax.random.key(seed), 10)
    previous = centred(key_list[0], (SPECTRAL_ANGLES, FREQ, GRID_ROW_TOTAL, NY), 2.0, 12.0, ((0, 2), (2, 16)))
    boundary = centred(key_list[1], (SPECTRAL_ANGLES, FREQ, NY), 1.0, 6.0, ((0, 2),), jnp.float32)
    row_coupling = draw_row_coupling(jax.random.fold_in(key_list[9], 71), 0)
    cross_gain = draw_cross_gain(jax.random.fold_in(key_list[9], 71), 0)
    block_inverse = draw_block_inverse(jax.random.fold_in(key_list[9], 71), 0)
    quadrant = set_ends(jax.random.randint(key_list[5], (SPECTRAL_ANGLES,), 0, 4), jax.random.fold_in(key_list[5], 1), 0, 3).astype(jnp.int32)
    sea_mask = draw_sea_mask(jax.random.fold_in(key_list[9], 71), 0)
    wet_tiles = set_ends((jax.random.randint(key_list[7], (GRID_ROW_TOTAL, NY // BLOCK), 0, 4) < 3).astype(jnp.int32), jax.random.fold_in(key_list[7], 1), 0, 1)
    quad_coef = jnp.clip(jnp.exp(jax.random.uniform(key_list[8], (FREQ,), jnp.float32, math.log(0.05), math.log(0.5))), 0.05, 0.5)
    return dict(previous=previous, boundary=boundary, row_coupling=row_coupling, cross_gain=cross_gain, block_inverse=block_inverse, quadrant=quadrant, sea_mask=sea_mask, wet_tiles=wet_tiles, quad_coef=quad_coef)


highest = lax.Precision.HIGHEST


def higher_band(field):
    return jnp.concatenate([field[:, 1:], jnp.zeros_like(field[:, :1])], axis=1)


def lower_band(field):
    return jnp.concatenate([jnp.zeros_like(field[:, :1]), field[:, :-1]], axis=1)


def quad_terms(center, onward, against, coefficients):
    nonlinear = center * center * (onward + against) - 2.0 * center * onward * against
    return coefficients[None, :, None, None] * nonlinear


def full_source(spectra, coefficients):
    energy = spectra.astype(jnp.float32)
    onward = higher_band(jnp.roll(energy, -SHIFT, axis=0))
    against = lower_band(jnp.roll(energy, SHIFT, axis=0))
    return quad_terms(energy, onward, against, coefficients)


def reference(previous, boundary, row_coupling, cross_gain, block_inverse, quadrant, sea_mask, wet_tiles, quad_coef):
    sea_cells = sea_mask.astype(jnp.float32)

    def sweep_one(members):
        prior, inflow, coupling, gain, inverse, corner = members
        couple = coupling * sea_cells
        forcing = sea_cells[None] * (1.0 - coupling)[None] * prior.astype(jnp.float32)
        rows_first = (couple, jnp.moveaxis(forcing, 1, 0))

        def advance(state_in, member):
            state_out = member[0][None] * state_in + member[1]
            return state_out, state_out

        _, onward = lax.scan(advance, inflow, rows_first)
        _, against = lax.scan(advance, inflow, rows_first, reverse=True)
        swept_rows = jnp.where(corner % 2 == 1, against, onward)
        sideways = corner // 2 == 1
        flipped = jnp.where(sideways, jnp.flip(swept_rows, -1), swept_rows)
        blocks = flipped.reshape(GRID_ROW_TOTAL, FREQ, NY // BLOCK, BLOCK)
        solved = jnp.einsum('ij,xfkj->xfki', inverse, blocks, precision=highest)
        pieces = [solved[:, :, 0]]
        for section in range(1, NY // BLOCK):
            pieces.append(solved[:, :, section] + gain * pieces[-1][..., -1:] * inverse[:, 0])
        settled = jnp.stack(pieces, 2).reshape(GRID_ROW_TOTAL, FREQ, NY)
        settled = jnp.where(sideways, jnp.flip(settled, -1), settled) * sea_cells[:, None, :]
        return jnp.moveaxis(settled, 0, 1)

    settled = lax.map(sweep_one, (previous, boundary, row_coupling, cross_gain, block_inverse, quadrant))
    rounded = lax.optimization_barrier(settled.astype(jnp.bfloat16))
    grouped = jnp.moveaxis(rounded.reshape(SPECTRAL_ANGLES, FREQ, GRID_ROW_TOTAL // CX, CX, NY), 2, 0)
    source = lax.map(lambda row_group: full_source(row_group, quad_coef).astype(jnp.bfloat16), grouped)
    source = jnp.moveaxis(source, 0, 2).reshape(SPECTRAL_ANGLES, FREQ, GRID_ROW_TOTAL, NY)
    source = lax.optimization_barrier(source)
    wet_cells = jnp.repeat(wet_tiles.astype(jnp.float32), BLOCK, axis=1)
    return (settled + wet_cells[None, None] * source.astype(jnp.float32)).astype(jnp.bfloat16)
```

```python
import functools

import jax
import jax.numpy as jnp
from jax import lax
from jax.experimental import pallas as pl
from jax.experimental.pallas import tpu as pltpu
from jax.sharding import PartitionSpec as P

SHIFT = 2
GROUP = 8
f32 = jnp.float32
bf16 = jnp.bfloat16
MESH = pl.DeviceIdType.MESH
VMEM_BYTES = 48 * 1024 * 1024


def cost(microseconds):
    return pl.CostEstimate(
        flops=0, bytes_accessed=int(microseconds * 3_000_000), transcendentals=0
    )


def weights(coupling, sea):
    return coupling * sea, sea * (1.0 - coupling)


def visit_order(shape, backward):
    row = lax.broadcasted_iota(jnp.int32, shape, 0)
    return shape[0] - 1 - row if backward else row


def rolled(x, steps, backward):
    rows = x.shape[0]
    return pltpu.roll(x, (rows - steps if backward else steps) % rows, 0)


def compose_kernel(quadrant, previous, coupling, sea, gain, state):
    d = pl.program_id(0)
    bands = previous.shape[1]

    def run(backward):
        couple, weight = weights(coupling[0], sea[...])
        rows = couple.shape[0]
        order = visit_order(couple.shape, backward)
        after = jnp.where(order < rows - 1, rolled(couple, rows - 1, backward), 1.0)
        span = 1
        while span < rows - 1:
            after = after * jnp.where(order < rows - span, rolled(after, rows - span, backward), 1.0)
            span *= 2
        gain[0] = jnp.sum(jnp.where(order == 0, couple * after, 0.0), axis=0, keepdims=True)
        total = weight * after

        def group(q, _):
            values = previous[0, pl.ds(q * GROUP, GROUP)].astype(f32)
            state[q, 0] = jnp.sum(values * total[None], axis=1)
            return 0

        lax.fori_loop(0, bands // GROUP, group, 0)

    pl.when(quadrant[d] % 2 == 0)(lambda: run(False))
    pl.when(quadrant[d] % 2 == 1)(lambda: run(True))


def compose_rows(quadrant, previous, coupling, sea):
    dirs, bands, rows, columns = previous.shape
    groups = bands // GROUP
    return pl.pallas_call(
        compose_kernel,
        grid=(dirs,),
        in_specs=[
            pl.BlockSpec(memory_space=pltpu.SMEM),
            pl.BlockSpec((1, bands, rows, columns), lambda d: (d, 0, 0, 0)),
            pl.BlockSpec((1, rows, columns), lambda d: (d, 0, 0)),
            pl.BlockSpec((rows, columns), lambda d: (0, 0)),
        ],
        out_specs=[
            pl.BlockSpec((1, 1, columns), lambda d: (d, 0, 0)),
            pl.BlockSpec((groups, 1, GROUP, columns), lambda d: (0, d, 0, 0)),
        ],
        out_shape=[
            jax.ShapeDtypeStruct((dirs, 1, columns), f32),
            jax.ShapeDtypeStruct((groups, dirs, GROUP, columns), f32),
        ],
        cost_estimate=cost(5),
        name="compose_rows",
    )(quadrant, previous, coupling, sea)


HALO_ARRAYS = 4


def scan_kernel(
    count, dir_count, chunks, gain, state, boundary, backward, *refs
):
    shared, refs = refs[:HALO_ARRAYS], refs[HALO_ARRAYS:]
    out, refs = refs[0], refs[1:]
    halos, refs = (refs[:HALO_ARRAYS], refs[HALO_ARRAYS : 2 * HALO_ARRAYS]), refs[2 * HALO_ARRAYS :]
    (
    gains, got_core, half_total, got_pair, plane, chain_in, chain_out, pair_in, pair_out, core_out,
    gain_send, gain_recv, core_send, core_recv, pair_send, pair_recv,
    chain_send, chain_recv, back_send, back_recv, last_send, last_recv, halo_send, halo_recv,
    ) = refs
    me = lax.axis_index("rows")
    c, x, z = me % 2, (me // 2) % 2, me // 4
    depth = count // 4
    core_peer = me + 1 - 2 * c
    pair_peer = me + 2 - 4 * x
    cross_peer = core_peer + 2 - 4 * x
    dirs = gain.shape[0]
    size = dirs // chunks
    peers = (core_peer, pair_peer, cross_peer)

    def part(j):
        return pl.ds(j * size, size)

    barrier = pltpu.get_barrier_semaphore()
    for peer in peers:
        pl.semaphore_signal(barrier, inc=1, device_id={"rows": peer}, device_id_type=MESH)

    @pl.when(z > 0)
    def _():
        pl.semaphore_signal(barrier, inc=1, device_id={"rows": me - 4}, device_id_type=MESH)

    @pl.when(z < depth - 1)
    def _():
        pl.semaphore_signal(barrier, inc=1, device_id={"rows": me + 4}, device_id_type=MESH)

    mine = lax.axis_index("dirs")
    higher, lower = (mine + 1) % dir_count, (mine + dir_count - 1) % dir_count
    neighbours = (higher, lower) if dir_count > 2 else (higher,)
    for peer in neighbours:
        pl.semaphore_signal(barrier, inc=1, device_id={"dirs": peer}, device_id_type=MESH)
    pl.semaphore_wait(
        barrier, 3 + len(neighbours) + (z > 0).astype(jnp.int32) + (z < depth - 1).astype(jnp.int32)
    )

    def remote(src, dst, send, recv, peer):
        return pltpu.make_async_remote_copy(
            src_ref=src, dst_ref=dst, send_sem=send, recv_sem=recv,
            device_id={"rows": peer}, device_id_type=MESH,
        )

    gain_copies = [
        remote(gain, gains.at[i], gain_send.at[i], gain_recv.at[i], peer) for i, peer in enumerate(peers)
    ]
    core_copies = [
        remote(state.at[1 - c, :, part(j)], got_core.at[:, part(j)], core_send.at[j], core_recv.at[j], core_peer)
        for j in range(chunks)
    ]
    pair_copies = [
        remote(half_total.at[1 - x, part(j)], got_pair.at[part(j)], pair_send.at[j], pair_recv.at[j], pair_peer)
        for j in range(chunks)
    ]
    back_copies = [
        remote(pair_out.at[part(j)], pair_in.at[x, part(j)], back_send.at[j], back_recv.at[j], pair_peer)
        for j in range(chunks)
    ]
    last_copies = [
        remote(core_out.at[:, part(j)], out.at[c, :, part(j)], last_send.at[j], last_recv.at[j], core_peer)
        for j in range(chunks)
    ]

    for copy in gain_copies:
        copy.start()
    for copy in core_copies:
        copy.start()
    halo_copies = []
    for way, (peer, start) in enumerate(((lower, 0), (higher, dirs - SHIFT))):
        for i, array in enumerate(shared):
            halo_copies.append(
                pltpu.make_async_remote_copy(
                    src_ref=array.at[pl.ds(start, SHIFT)], dst_ref=halos[way][i],
                    send_sem=halo_send.at[way, i], recv_sem=halo_recv.at[way, i],
                    device_id={"dirs": peer}, device_id_type=MESH,
                )
            )
            halo_copies[-1].start()

    back = backward[...]
    c_bit, x_bit = c.astype(f32), x.astype(f32)
    core_after = c_bit + back - 2.0 * c_bit * back
    pair_after = x_bit + back - 2.0 * x_bit * back
    for copy in gain_copies:
        copy.wait_recv()
    core_mine, core_theirs = gain[...], gains[0]
    pair_mine, pair_theirs = core_mine * core_theirs, gains[1] * gains[2]
    plane_gain = pair_mine * pair_theirs

    def total(after, mine, theirs):
        return after * mine + (1.0 - after), (1.0 - after) * theirs + after

    core_a, core_b = total(core_after, core_mine, core_theirs)
    pair_a, pair_b = total(pair_after, pair_mine, pair_theirs)

    def cut(v, j):
        return v[j * size : (j + 1) * size]

    for j in range(chunks):
        core_copies[j].wait_recv()
        half_total[:, part(j)] = (
            cut(core_a, j)[None] * got_core[:, part(j)] + cut(core_b, j)[None] * state[c, :, part(j)]
        )
        pair_copies[j].start()
    for j in range(chunks):
        pair_copies[j].wait_recv()
        plane[part(j)] = cut(pair_a, j) * got_pair[part(j)] + cut(pair_b, j) * half_total[x, part(j)]

    upper = (2 * z >= depth).astype(jnp.int32)
    mine_at = 2 * c + x

    def chain(j, way):
        step = 1 - 2 * way
        has_before = jnp.where(way == 0, z > 0, z < depth - 1)
        has_after = jnp.where(way == 0, z < depth - 1, z > 0)
        copy = remote(
            chain_out.at[way, part(j)], chain_in.at[way, part(j)],
            chain_send.at[way, j], chain_recv.at[way, j], me + 4 * step,
        )

        @pl.when(has_before)
        def _():
            copy.wait_recv()

        @pl.when(jnp.logical_not(has_before))
        def _():
            chain_in[way, part(j)] = boundary[part(j), mine_at]

        @pl.when(has_after)
        def _():
            chain_out[way, part(j)] = cut(plane_gain, j) * chain_in[way, part(j)] + plane[part(j)]
            copy.start()

    def split(after, mine, theirs):
        return after * theirs + (1.0 - after), (1.0 - after) * mine + after

    pair_p, pair_q = split(pair_after, pair_mine, pair_theirs)
    core_p, core_q = split(core_after, core_mine, core_theirs)
    for j in range(chunks):
        chain(j, upper)
        chain(j, 1 - upper)
        entering = jnp.where(cut(back, j) > 0.5, chain_in[1, part(j)], chain_in[0, part(j)])
        pair_out[part(j)] = cut(pair_q, j) * entering + (1.0 - cut(pair_after, j)) * half_total[x, part(j)]
        back_copies[j].start()
        pair_in[x, part(j)] = cut(pair_p, j) * entering + cut(pair_after, j) * got_pair[part(j)]
    for j in range(chunks):
        back_copies[j].wait_recv()
        entering = pair_in[:, part(j)]
        core_out[:, part(j)] = (
            cut(core_q, j)[None] * entering + (1.0 - cut(core_after, j))[None] * state[c, :, part(j)]
        )
        last_copies[j].start()
        out[c, :, part(j)] = cut(core_p, j)[None] * entering + cut(core_after, j)[None] * got_core[:, part(j)]
    for j in range(chunks):
        last_copies[j].wait_recv()
    for copy in halo_copies:
        copy.wait_recv()
    for copy in halo_copies + gain_copies + core_copies + pair_copies + back_copies + last_copies:
        copy.wait_send()

    def drain(j, way):
        copy = remote(
            chain_out.at[way, part(j)], chain_in.at[way, part(j)],
            chain_send.at[way, j], chain_recv.at[way, j], me + 4 * (1 - 2 * way),
        )

        @pl.when(z < depth - 1 if way == 0 else z > 0)
        def _():
            copy.wait_send()

    for j in range(chunks):
        drain(j, 0)
        drain(j, 1)


def scan_devices(count, dir_count, gain, state, boundary, backward, shared):
    groups, dirs, _, columns = state.shape
    chunks = 3 if dirs % 3 == 0 else 1
    quarter = groups // 4 * GROUP
    state = state.reshape(2, 2, dirs, quarter, columns)
    boundary = boundary.reshape(dirs, 4, quarter, columns)
    vmem = pl.BlockSpec(memory_space=pltpu.VMEM)
    part = (dirs, quarter, columns)
    dma = pltpu.SemaphoreType.DMA
    anywhere = pl.BlockSpec(memory_space=pl.ANY)
    halos = [jax.ShapeDtypeStruct((SHIFT,) + a.shape[1:], a.dtype) for a in shared] * 2
    out, *halos = pl.pallas_call(
        functools.partial(scan_kernel, count, dir_count, chunks),
        in_specs=[vmem] * 4 + [anywhere] * HALO_ARRAYS,
        out_specs=[vmem] + [anywhere] * (2 * HALO_ARRAYS),
        out_shape=[jax.ShapeDtypeStruct(state.shape, f32)] + halos,
        scratch_shapes=[
            pltpu.VMEM((3, dirs, 1, columns), f32),
            pltpu.VMEM((2,) + part, f32),
            pltpu.VMEM((2,) + part, f32),
            pltpu.VMEM(part, f32),
            pltpu.VMEM(part, f32),
            pltpu.VMEM((2,) + part, f32),
            pltpu.VMEM((2,) + part, f32),
            pltpu.VMEM((2,) + part, f32),
            pltpu.VMEM(part, f32),
            pltpu.VMEM((2,) + part, f32),
            dma((3,)), dma((3,)),
            dma((chunks,)), dma((chunks,)),
            dma((chunks,)), dma((chunks,)),
            dma((2, chunks)), dma((2, chunks)),
            dma((chunks,)), dma((chunks,)),
            dma((chunks,)), dma((chunks,)),
            dma((2, HALO_ARRAYS)), dma((2, HALO_ARRAYS)),
        ],
        compiler_params=pltpu.CompilerParams(
            collective_id=0, has_side_effects=True, vmem_limit_bytes=VMEM_BYTES
        ),
        cost_estimate=cost(35),
        name="scan_devices",
    )(gain, state, boundary, backward, *shared)
    return out.reshape(groups, dirs, GROUP, columns), halos[:HALO_ARRAYS], halos[HALO_ARRAYS:]


def settle_kernel(quadrant, previous, coupling, sea, entering, matrix, carry, *rest):
    swept = rest[-1]
    outs = rest[:-1]
    d = pl.program_id(0)
    _, bands, rows, columns = previous.shape
    block = carry.shape[-1]
    pieces = columns // block

    def sweep(backward):
        couple, weight = weights(coupling[0], sea[...])
        order = visit_order(couple.shape, backward)
        first = jnp.where(order == 0, couple, 0.0)
        spans, reach, span = [], couple, 1
        while span < rows:
            spans.append((span, jnp.where(order >= span, reach, 0.0)))
            reach = jnp.where(order >= span, reach * rolled(reach, span, backward), reach)
            span *= 2

        def group(q, _):
            inflow = entering[q, 0]
            for r in range(GROUP):
                value = weight * previous[0, q * GROUP + r].astype(f32) + first * inflow[r : r + 1]
                for span, factor in spans:
                    value = value + factor * rolled(value, span, backward)
                swept[q * GROUP + r] = value
            return 0

        lax.fori_loop(0, bands // GROUP, group, 0)

    pl.when(quadrant[d] % 2 == 0)(lambda: sweep(False))
    pl.when(quadrant[d] % 2 == 1)(lambda: sweep(True))

    def columns_solve(sideways):
        upper = matrix[0]
        whole = jnp.concatenate(
            [upper, jnp.concatenate([upper[:, :block], jnp.zeros((block, block), bf16)], axis=1)], axis=0
        )
        before = None
        for k in range(pieces - 1, -1, -1) if sideways else range(pieces):
            here = slice(k * block, (k + 1) * block)
            x = swept[:, :, here].reshape(bands * rows, block)
            high = x.astype(bf16)
            low = (x - high.astype(f32)).astype(bf16)
            both = jnp.dot(
                jnp.concatenate([high, low], axis=1), whole, preferred_element_type=f32
            )
            y = both[:, :block] + both[:, block:]
            if before is not None:
                last = before[:, :1] if sideways else before[:, block - 1 :]
                y = y + last * carry[0]
            before = y
            masked = y.reshape(bands, rows, block) * sea[:, here][None]
            outs[0][0, :, :, here] = masked.astype(bf16)
            if len(outs) > 1:
                outs[1][0, :, :, here] = masked

    pl.when(quadrant[d] // 2 == 0)(lambda: columns_solve(False))
    pl.when(quadrant[d] // 2 == 1)(lambda: columns_solve(True))


def settle(quadrant, previous, coupling, sea, entering, matrix, carry, keep):
    dirs, bands, rows, columns = previous.shape
    block = carry.shape[-1]
    field = pl.BlockSpec((1, bands, rows, columns), lambda d: (d, 0, 0, 0))
    kinds = [bf16, f32] if keep else [bf16]
    return pl.pallas_call(
        settle_kernel,
        grid=(dirs,),
        in_specs=[
            pl.BlockSpec(memory_space=pltpu.SMEM),
            field,
            pl.BlockSpec((1, rows, columns), lambda d: (d, 0, 0)),
            pl.BlockSpec((rows, columns), lambda d: (0, 0)),
            pl.BlockSpec((bands // GROUP, 1, GROUP, columns), lambda d: (0, d, 0, 0)),
            pl.BlockSpec((1, block, 2 * block), lambda d: (d, 0, 0)),
            pl.BlockSpec((1, 1, block), lambda d: (d, 0, 0)),
        ],
        out_specs=[field] * len(kinds),
        out_shape=[jax.ShapeDtypeStruct(previous.shape, kind) for kind in kinds],
        scratch_shapes=[pltpu.VMEM((bands, rows, columns), f32)],
        compiler_params=pltpu.CompilerParams(vmem_limit_bytes=VMEM_BYTES),
        cost_estimate=cost(dirs),
        name="settle_keep" if keep else "settle_halo",
    )(quadrant, previous, coupling, sea, entering, matrix, carry)


def source_kernel(dirs, coef, wet, settled, center, above, below, above_halo, below_halo, out):
    d = pl.program_id(0)
    bands = center.shape[1]

    def run(above, below):
        wet_cells = wet[...]

        def one(f, onward, against):
            energy = center[0, f].astype(f32)
            onward, against = onward.astype(f32), against.astype(f32)
            source = coef[f] * (
                energy * energy * (onward + against) - 2.0 * energy * onward * against
            )
            out[0, f] = (settled[0, f] + wet_cells * source.astype(bf16).astype(f32)).astype(bf16)

        nothing = jnp.zeros(wet.shape, f32)
        one(0, above[0, 1], nothing)
        one(bands - 1, nothing, below[0, bands - 2])

        def body(f, _):
            one(f, above[0, f + 1], below[0, f - 1])
            return 0

        lax.fori_loop(1, bands - 1, body, 0, unroll=6 if (bands - 2) % 6 == 0 else 1)

    top, low = d + SHIFT >= dirs, d < SHIFT
    for top_here in (False, True):
        for low_here in (False, True):
            pl.when((top == top_here) & (low == low_here))(
                functools.partial(
                    run, above_halo if top_here else above, below_halo if low_here else below
                )
            )


def add_source(coef, wet, settled, rounded, above_halo, below_halo):
    dirs, bands, rows, columns = rounded.shape
    shape = (1, bands, rows, columns)

    def at(place):
        return pl.BlockSpec(shape, lambda d: (place(d), 0, 0, 0))

    return pl.pallas_call(
        functools.partial(source_kernel, dirs),
        grid=(dirs,),
        in_specs=[
            pl.BlockSpec(memory_space=pltpu.SMEM),
            pl.BlockSpec((rows, columns), lambda d: (0, 0)),
            at(lambda d: d),
            at(lambda d: d),
            at(lambda d: jnp.minimum(d + SHIFT, dirs - 1)),
            at(lambda d: jnp.maximum(d - SHIFT, 0)),
            at(lambda d: jnp.maximum(d + SHIFT - dirs, 0)),
            at(lambda d: jnp.minimum(d, SHIFT - 1)),
        ],
        out_specs=at(lambda d: d),
        out_shape=jax.ShapeDtypeStruct(rounded.shape, bf16),
        compiler_params=pltpu.CompilerParams(vmem_limit_bytes=VMEM_BYTES),
        cost_estimate=cost(10),
        name="add_source",
    )(coef, wet, settled, rounded, rounded, rounded, above_halo, below_halo)


def on_device(
    row_devices, dir_devices,
    previous, boundary, row_coupling, cross_gain, block_inverse, quadrant, sea_mask, wet_tiles, quad_coef,
):
    dirs, bands, rows, columns = previous.shape
    block = block_inverse.shape[-1]
    sea = sea_mask.astype(f32)
    wet = jnp.repeat(wet_tiles.astype(f32), block, axis=1)
    up = [(i, (i + 1) % dir_devices) for i in range(dir_devices)]
    down = [(i, (i - 1) % dir_devices) for i in range(dir_devices)]

    def from_above(a):
        return lax.ppermute(a, "dirs", down)

    def from_below(a):
        return lax.ppermute(a, "dirs", up)

    sideways = quadrant // 2 == 1
    matrix = jnp.where(
        sideways[:, None, None], block_inverse, jnp.swapaxes(block_inverse, 1, 2)
    )
    carry = cross_gain[:, None] * jnp.where(
        sideways[:, None], block_inverse[:, block - 1], block_inverse[:, :, 0]
    )
    high = lax.reduce_precision(matrix, 8, 7)
    low = (matrix - high).astype(bf16)
    high = high.astype(bf16)
    paired = jnp.concatenate([high, low], 2)
    marked = jnp.concatenate(
        [carry, jnp.broadcast_to(quadrant.astype(f32)[:, None], carry.shape)], 1
    )[:, None, :]
    carry = carry[:, None, :]

    gain, state = compose_rows(quadrant, previous, row_coupling, sea)
    backward = jnp.broadcast_to((quadrant % 2).astype(f32)[:, None, None], (dirs, 1, columns))
    entering, above, below = scan_devices(
        row_devices, dir_devices, gain, state, boundary, backward,
        (previous, row_coupling, paired, marked),
    )
    enter_above = from_above(entering[:, :SHIFT])
    enter_below = from_below(entering[:, dirs - SHIFT :])

    rounded, settled = settle(
        quadrant, previous, row_coupling, sea, entering, paired, carry, True
    )

    def halo(parts, inflow):
        prior, coupling, half, marks = parts
        quad = marks[:, 0, block].astype(jnp.int32)
        return settle(quad, prior, coupling, sea, inflow, half, marks[:, :, :block], False)[0]

    above_halo = halo(above, enter_above)
    below_halo = halo(below, enter_below)
    return add_source(quad_coef, wet, settled, rounded, above_halo, below_halo)


def solution(mesh):
    in_specs = (
        P("dirs", None, "rows", None),
        P("dirs", None, None),
        P("dirs", "rows", None),
        P("dirs"),
        P("dirs", None, None),
        P("dirs"),
        P("rows", None),
        P("rows", None),
        P(),
    )
    out_specs = P("dirs", None, "rows", None)
    return jax.shard_map(
        functools.partial(on_device, mesh.shape["rows"], mesh.shape["dirs"]),
        mesh=mesh, in_specs=in_specs, out_specs=out_specs, check_vma=False,
    )
```

```python
import functools

import jax
import jax.numpy as jnp
from jax import lax
from jax.experimental import pallas as pl
from jax.experimental.pallas import tpu as pltpu
from jax.sharding import PartitionSpec as P

SHIFT = 2
f32 = jnp.float32
bf16 = jnp.bfloat16
MESH = pl.DeviceIdType.MESH
VMEM_BYTES = 48 * 1024 * 1024


def cost(microseconds):
    return pl.CostEstimate(
        flops=0, bytes_accessed=int(microseconds * 3_000_000), transcendentals=0
    )


def weights(coupling, sea):
    return coupling * sea, sea * (1.0 - coupling)


def visit_order(shape, backward):
    row = lax.broadcasted_iota(jnp.int32, shape, 0)
    return shape[0] - 1 - row if backward else row


def rolled(x, steps, backward):
    rows = x.shape[0]
    return pltpu.roll(x, (rows - steps if backward else steps) % rows, 0)


def row_weights(coupling, sea, backward):
    couple, weight = weights(coupling, sea)
    rows = couple.shape[0]
    order = visit_order(couple.shape, backward)
    after = jnp.where(order < rows - 1, rolled(couple, rows - 1, backward), 1.0)
    span = 1
    while span < rows - 1:
        after = after * jnp.where(order < rows - span, rolled(after, rows - span, backward), 1.0)
        span *= 2
    gain = jnp.sum(jnp.where(order == 0, couple * after, 0.0), axis=0, keepdims=True)
    return weight * after, gain


HALO_ARRAYS = 4


def scan_kernel(
    count, dir_count, chunks, boundary, sea_mask, previous, coupling, inverse, marks, out, *refs
):
    shared = (previous, coupling, inverse, marks)
    halos, refs = refs[:HALO_ARRAYS], refs[HALO_ARRAYS:]
    enter_halo, refs = refs[0], refs[1:]
    (
        gain, state, shares,
        gains, got_core, half_total, got_pair, plane, chain_in, chain_out, pair_in, pair_out, core_out,
        gain_send, gain_recv, core_send, core_recv, pair_send, pair_recv,
        chain_send, chain_recv, back_send, back_recv, last_send, last_recv, halo_send, halo_recv,
        enter_send, enter_recv,
    ) = refs
    me = lax.axis_index("rows")
    c, x, z = me % 2, (me // 2) % 2, me // 4
    depth = count // 4
    core_peer = me + 1 - 2 * c
    pair_peer = me + 2 - 4 * x
    cross_peer = core_peer + 2 - 4 * x
    dirs = gain.shape[0]
    size = dirs // chunks
    peers = (core_peer, pair_peer, cross_peer)

    def part(j):
        return pl.ds(j * size, size)

    barrier = pltpu.get_barrier_semaphore()
    for peer in peers:
        pl.semaphore_signal(barrier, inc=1, device_id={"rows": peer}, device_id_type=MESH)

    @pl.when(z > 0)
    def _():
        pl.semaphore_signal(barrier, inc=1, device_id={"rows": me - 4}, device_id_type=MESH)

    @pl.when(z < depth - 1)
    def _():
        pl.semaphore_signal(barrier, inc=1, device_id={"rows": me + 4}, device_id_type=MESH)

    mine = lax.axis_index("dirs")
    higher, lower = (mine + 1) % dir_count, (mine + dir_count - 1) % dir_count
    neighbours = (higher, lower) if dir_count > 2 else (higher,)
    for peer in neighbours:
        pl.semaphore_signal(barrier, inc=1, device_id={"dirs": peer}, device_id_type=MESH)
    pl.semaphore_wait(
        barrier, 3 + len(neighbours) + (z > 0).astype(jnp.int32) + (z < depth - 1).astype(jnp.int32)
    )

    def remote(src, dst, send, recv, peer):
        return pltpu.make_async_remote_copy(
            src_ref=src, dst_ref=dst, send_sem=send, recv_sem=recv,
            device_id={"rows": peer}, device_id_type=MESH,
        )

    gain_copies = [
        remote(gain, gains.at[i], gain_send.at[i], gain_recv.at[i], peer) for i, peer in enumerate(peers)
    ]
    core_copies = [
        remote(state.at[1 - c, :, part(j)], got_core.at[:, part(j)], core_send.at[j], core_recv.at[j], core_peer)
        for j in range(chunks)
    ]
    pair_copies = [
        remote(half_total.at[1 - x, part(j)], got_pair.at[part(j)], pair_send.at[j], pair_recv.at[j], pair_peer)
        for j in range(chunks)
    ]
    back_copies = [
        remote(pair_out.at[part(j)], pair_in.at[x, part(j)], back_send.at[j], back_recv.at[j], pair_peer)
        for j in range(chunks)
    ]
    last_copies = [
        remote(core_out.at[:, part(j)], out.at[c, :, part(j)], last_send.at[j], last_recv.at[j], core_peer)
        for j in range(chunks)
    ]

    halo_copies, enter_copies = [], []
    for way, (peer, start, to) in enumerate(((lower, 0, SHIFT), (higher, dirs - SHIFT, 0))):
        enter_copies.append(
            pltpu.make_async_remote_copy(
                src_ref=out.at[:, :, pl.ds(start, SHIFT)], dst_ref=enter_halo.at[:, :, pl.ds(to, SHIFT)],
                send_sem=enter_send.at[way], recv_sem=enter_recv.at[way],
                device_id={"dirs": peer}, device_id_type=MESH,
            )
        )
        for i, array in enumerate(shared):
            halo_copies.append(
                pltpu.make_async_remote_copy(
                    src_ref=array.at[pl.ds(start, SHIFT)], dst_ref=halos[i].at[pl.ds(to, SHIFT)],
                    send_sem=halo_send.at[way, i], recv_sem=halo_recv.at[way, i],
                    device_id={"dirs": peer}, device_id_type=MESH,
                )
            )
            halo_copies[-1].start()

    flags = marks[:, 1:2, :]
    flags = flags - 2.0 * jnp.floor(0.5 * flags)
    back = jnp.concatenate([flags] * (gain.shape[-1] // flags.shape[-1]), axis=2)
    sea = sea_mask[...].astype(f32)
    for d in range(dirs):
        onward, onward_gain = row_weights(coupling[d], sea, False)
        against, _ = row_weights(coupling[d], sea, True)
        shares[d] = jnp.where(back[d] > 0.5, against, onward)
        gain[d] = onward_gain
    for copy in gain_copies:
        copy.start()
    order = [0] + list(range(chunks - 1, 0, -1))
    for j in order:

        def compose(d, _):
            share = shares[d]
            for h in range(2):
                for q in range(2):
                    band = (2 * h + q) * state.shape[3]
                    values = previous[d, band : band + state.shape[3]].astype(f32)
                    state[h, q, d] = jnp.sum(values * share[None], axis=1)
            return 0

        lax.fori_loop(j * size, (j + 1) * size, compose, 0)
        core_copies[j].start()
    c_bit, x_bit = c.astype(f32), x.astype(f32)
    core_after = c_bit + back - 2.0 * c_bit * back
    pair_after = x_bit + back - 2.0 * x_bit * back
    for copy in gain_copies:
        copy.wait_recv()
    core_mine, core_theirs = gain[...], gains[0]
    pair_mine, pair_theirs = core_mine * core_theirs, gains[1] * gains[2]
    plane_gain = pair_mine * pair_theirs

    def total(after, mine, theirs):
        return after * mine + (1.0 - after), (1.0 - after) * theirs + after

    core_a, core_b = total(core_after, core_mine, core_theirs)
    pair_a, pair_b = total(pair_after, pair_mine, pair_theirs)

    def cut(v, j):
        return v[j * size : (j + 1) * size]

    for j in order:
        core_copies[j].wait_recv()
        half_total[:, part(j)] = (
            cut(core_a, j)[None] * got_core[:, part(j)] + cut(core_b, j)[None] * state[c, :, part(j)]
        )
        pair_copies[j].start()
    for j in order:
        pair_copies[j].wait_recv()
        plane[part(j)] = cut(pair_a, j) * got_pair[part(j)] + cut(pair_b, j) * half_total[x, part(j)]

    upper = (2 * z >= depth).astype(jnp.int32)
    mine_at = 2 * c + x

    def chain(j, way):
        step = 1 - 2 * way
        has_before = jnp.where(way == 0, z > 0, z < depth - 1)
        has_after = jnp.where(way == 0, z < depth - 1, z > 0)
        copy = remote(
            chain_out.at[way, part(j)], chain_in.at[way, part(j)],
            chain_send.at[way, j], chain_recv.at[way, j], me + 4 * step,
        )

        @pl.when(has_before)
        def _():
            copy.wait_recv()

        @pl.when(jnp.logical_not(has_before))
        def _():
            chain_in[way, part(j)] = boundary[part(j), mine_at]

        @pl.when(has_after)
        def _():
            chain_out[way, part(j)] = cut(plane_gain, j) * chain_in[way, part(j)] + plane[part(j)]
            copy.start()

    def split(after, mine, theirs):
        return after * theirs + (1.0 - after), (1.0 - after) * mine + after

    pair_p, pair_q = split(pair_after, pair_mine, pair_theirs)
    core_p, core_q = split(core_after, core_mine, core_theirs)
    for j in order:
        chain(j, upper)
        chain(j, 1 - upper)
        entering = jnp.where(cut(back, j) > 0.5, chain_in[1, part(j)], chain_in[0, part(j)])
        pair_out[part(j)] = cut(pair_q, j) * entering + (1.0 - cut(pair_after, j)) * half_total[x, part(j)]
        back_copies[j].start()
        pair_in[x, part(j)] = cut(pair_p, j) * entering + cut(pair_after, j) * got_pair[part(j)]
    for j in order:
        back_copies[j].wait_recv()
        entering = pair_in[:, part(j)]
        core_out[:, part(j)] = (
            cut(core_q, j)[None] * entering + (1.0 - cut(core_after, j))[None] * state[c, :, part(j)]
        )
        last_copies[j].start()
        out[c, :, part(j)] = cut(core_p, j)[None] * entering + cut(core_after, j)[None] * got_core[:, part(j)]
    for j in order:
        last_copies[j].wait_recv()
        if j == 0:
            enter_copies[0].start()
        if j == chunks - 1:
            enter_copies[1].start()
    for copy in halo_copies + enter_copies:
        copy.wait_recv()
    for copy in halo_copies + enter_copies + gain_copies + core_copies + pair_copies + back_copies + last_copies:
        copy.wait_send()

    def drain(j, way):
        copy = remote(
            chain_out.at[way, part(j)], chain_in.at[way, part(j)],
            chain_send.at[way, j], chain_recv.at[way, j], me + 4 * (1 - 2 * way),
        )

        @pl.when(z < depth - 1 if way == 0 else z > 0)
        def _():
            copy.wait_send()

    for j in range(chunks):
        drain(j, 0)
        drain(j, 1)


def scan_devices(count, dir_count, boundary, sea_mask, previous, coupling, inverse, marks):
    dirs, bands, _, columns = previous.shape
    chunks = 1
    quarter = bands // 4
    boundary = boundary.reshape(dirs, 4, quarter, columns)
    vmem = pl.BlockSpec(memory_space=pltpu.VMEM)
    part = (dirs, quarter, columns)
    dma = pltpu.SemaphoreType.DMA
    anywhere = pl.BlockSpec(memory_space=pl.ANY)
    shared = (previous, coupling, inverse, marks)
    halos = [jax.ShapeDtypeStruct((2 * SHIFT,) + a.shape[1:], a.dtype) for a in shared]
    out, *halos = pl.pallas_call(
        functools.partial(scan_kernel, count, dir_count, chunks),
        in_specs=[vmem, vmem, vmem, vmem, anywhere, vmem],
        out_specs=[vmem] + [anywhere] * HALO_ARRAYS + [vmem],
        out_shape=[jax.ShapeDtypeStruct((2, 2) + part, f32)]
        + halos
        + [jax.ShapeDtypeStruct((2, 2, 2 * SHIFT, quarter, columns), f32)],
        scratch_shapes=[
            pltpu.VMEM((dirs, 1, columns), f32),
            pltpu.VMEM((2, 2) + part, f32),
            pltpu.VMEM(coupling.shape, f32),
            pltpu.VMEM((3, dirs, 1, columns), f32),
            pltpu.VMEM((2,) + part, f32),
            pltpu.VMEM((2,) + part, f32),
            pltpu.VMEM(part, f32),
            pltpu.VMEM(part, f32),
            pltpu.VMEM((2,) + part, f32),
            pltpu.VMEM((2,) + part, f32),
            pltpu.VMEM((2,) + part, f32),
            pltpu.VMEM(part, f32),
            pltpu.VMEM((2,) + part, f32),
            dma((3,)), dma((3,)),
            dma((chunks,)), dma((chunks,)),
            dma((chunks,)), dma((chunks,)),
            dma((2, chunks)), dma((2, chunks)),
            dma((chunks,)), dma((chunks,)),
            dma((chunks,)), dma((chunks,)),
            dma((2, HALO_ARRAYS)), dma((2, HALO_ARRAYS)),
            dma((2,)), dma((2,)),
        ],
        compiler_params=pltpu.CompilerParams(
            collective_id=0, has_side_effects=True, vmem_limit_bytes=VMEM_BYTES
        ),
        cost_estimate=cost(35),
        name="scan_devices",
    )(boundary, sea_mask, previous, coupling, inverse, marks)
    return (
        out.reshape(4, dirs, quarter, columns),
        halos[:HALO_ARRAYS],
        halos[HALO_ARRAYS].reshape(4, 2 * SHIFT, quarter, columns),
    )


def step_kernel(
    dirs, quadrant, cross_gain, halo_marks, coef, sea_mask, wet_tiles,
    previous, coupling, inverse, entering,
    halo_previous, halo_coupling, halo_inverse, halo_entering,
    out, swept, rounded, settled, sea, wet,
):
    t = pl.program_id(0)
    _, bands, rows, columns = previous.shape
    block = inverse.shape[-1]
    pieces = columns // block
    quarter = bands // 4

    @pl.when(t == 0)
    def _():
        sea[...] = sea_mask[...].astype(f32)
        for k in range(pieces):
            flag = wet_tiles[:, k : k + 1].astype(f32)
            wet[:, k * block : (k + 1) * block] = jnp.broadcast_to(flag, (rows, block))

    def sweep(previous, coupling, entering, backward):
        couple, weight = weights(coupling[0], sea[...])
        order = visit_order(couple.shape, backward)
        first = jnp.where(order == 0, couple, 0.0)
        spans, reach, span = [], couple, 1
        while span < rows:
            spans.append((span, jnp.where(order >= span, reach, 0.0)))
            reach = jnp.where(order >= span, reach * rolled(reach, span, backward), reach)
            span *= 2

        def group(q, _):
            inflow = entering[q, 0]
            for r in range(quarter):
                value = weight * previous[0, q * quarter + r].astype(f32) + first * inflow[r : r + 1]
                for span, factor in spans:
                    value = value + factor * rolled(value, span, backward)
                swept[q * quarter + r] = value
            return 0

        lax.fori_loop(0, 4, group, 0)

    def columns_solve(inverse, gain, slot, keep, sideways):
        matrix = inverse[0] if sideways else inverse[0].T
        carry = gain * (matrix[block - 1 :] if sideways else matrix[:1])
        high = matrix.astype(bf16)
        low = (matrix - high.astype(f32)).astype(bf16)
        whole = jnp.concatenate(
            [
                jnp.concatenate([high, low], axis=1),
                jnp.concatenate([high, jnp.zeros_like(low)], axis=1),
            ],
            axis=0,
        )
        before = None
        for k in range(pieces - 1, -1, -1) if sideways else range(pieces):
            here = slice(k * block, (k + 1) * block)
            x = swept[:, :, here].reshape(bands * rows, block)
            upper = x.astype(bf16)
            lower = (x - upper.astype(f32)).astype(bf16)
            both = jnp.dot(
                jnp.concatenate([upper, lower], axis=1), whole, preferred_element_type=f32
            )
            y = both[:, :block] + both[:, block:]
            if before is not None:
                y = y + (before[:, :1] if sideways else before[:, block - 1 :]) * carry
            before = y
            masked = y.reshape(bands, rows, block) * sea[:, here][None]
            rounded[slot, :, :, here] = masked.astype(bf16)
            if keep:
                settled[t, :, :, here] = masked

    def settle(previous, coupling, inverse, entering, corner, gain, slot, keep):
        for flag in (0, 1):
            pl.when(corner % 2 == flag)(
                functools.partial(sweep, previous, coupling, entering, flag == 1)
            )
        for flag in (0, 1):
            pl.when(corner // 2 == flag)(
                functools.partial(columns_solve, inverse, gain, slot, keep, flag == 1)
            )

    @pl.when(t < dirs)
    def _():
        at = jnp.minimum(t, dirs - 1)
        settle(previous, coupling, inverse, entering, quadrant[at], cross_gain[at], t + SHIFT, True)

    @pl.when(t >= dirs)
    def _():
        at = jnp.maximum(t - dirs, 0)
        settle(
            halo_previous, halo_coupling, halo_inverse, halo_entering,
            halo_marks[at, 1, 0].astype(jnp.int32), halo_marks[at, 0, 0],
            jnp.where(t < dirs + SHIFT, t - dirs, t), False,
        )

    @pl.when((t >= dirs) | (t >= 2 * SHIFT))
    def _():
        d = source_place(dirs, t)
        wet_cells = wet[...]

        def one(f, onward, against):
            energy = rounded[d + SHIFT, f].astype(f32)
            source = coef[f] * (
                energy * energy * (onward + against) - 2.0 * energy * onward * against
            )
            out[0, f] = (settled[d, f] + wet_cells * source.astype(bf16).astype(f32)).astype(bf16)

        def above(f):
            return rounded[d + 2 * SHIFT, f + 1].astype(f32)

        def below(f):
            return rounded[d, f - 1].astype(f32)

        nothing = jnp.zeros(wet.shape, f32)
        one(0, above(0), nothing)
        one(bands - 1, nothing, below(bands - 1))

        def body(f, _):
            one(f, above(f), below(f))
            return 0

        lax.fori_loop(1, bands - 1, body, 0, unroll=6 if (bands - 2) % 6 == 0 else 1)


def source_place(dirs, t):
    inner = jnp.clip(t - SHIFT, SHIFT, dirs - SHIFT - 1) if dirs > 2 * SHIFT else 0
    edge = jnp.where(t < dirs + SHIFT, t - dirs, t - 2 * SHIFT)
    return jnp.where(t < dirs, inner, edge)


def add_step(
    quadrant, cross_gain, quad_coef, sea_mask, wet_tiles,
    previous, coupling, inverse, entering, halos, halo_entering,
):
    dirs, bands, rows, columns = previous.shape
    halo_previous, halo_coupling, halo_inverse, halo_marks = halos
    smem = pl.BlockSpec(memory_space=pltpu.SMEM)

    def own(t):
        return jnp.minimum(t, dirs - 1)

    def halo(t):
        return jnp.maximum(t - dirs, 0)

    def specs(at):
        return [
            pl.BlockSpec((1,) + previous.shape[1:], lambda t: (at(t), 0, 0, 0)),
            pl.BlockSpec((1,) + coupling.shape[1:], lambda t: (at(t), 0, 0)),
            pl.BlockSpec((1,) + inverse.shape[1:], lambda t: (at(t), 0, 0)),
            pl.BlockSpec((4, 1) + entering.shape[2:], lambda t: (0, at(t), 0, 0)),
        ]

    return pl.pallas_call(
        functools.partial(step_kernel, dirs),
        grid=(dirs + 2 * SHIFT,),
        in_specs=[
            smem, smem, smem, smem,
            pl.BlockSpec(sea_mask.shape, lambda t: (0, 0)),
            pl.BlockSpec(wet_tiles.shape, lambda t: (0, 0)),
        ]
        + specs(own)
        + specs(halo),
        out_specs=pl.BlockSpec(
            (1,) + previous.shape[1:], lambda t: (source_place(dirs, t), 0, 0, 0)
        ),
        out_shape=jax.ShapeDtypeStruct(previous.shape, bf16),
        scratch_shapes=[
            pltpu.VMEM((bands, rows, columns), f32),
            pltpu.VMEM((dirs + 2 * SHIFT, bands, rows, columns), bf16),
            pltpu.VMEM((dirs, bands, rows, columns), f32),
            pltpu.VMEM((rows, columns), f32),
            pltpu.VMEM((rows, columns), f32),
        ],
        compiler_params=pltpu.CompilerParams(vmem_limit_bytes=VMEM_BYTES),
        cost_estimate=cost(20),
        name="add_step",
    )(
        quadrant, cross_gain, halo_marks, quad_coef, sea_mask, wet_tiles,
        previous, coupling, inverse, entering,
        halo_previous, halo_coupling, halo_inverse, halo_entering,
    )


def on_device(
    row_devices, dir_devices,
    previous, boundary, row_coupling, cross_gain, block_inverse, quadrant, sea_mask, wet_tiles, quad_coef,
):
    dirs = previous.shape[0]
    block = block_inverse.shape[-1]
    marks = jnp.broadcast_to(
        jnp.stack([cross_gain, quadrant.astype(f32)], 1)[:, :, None], (dirs, 2, block)
    )
    entering, halos, halo_entering = scan_devices(
        row_devices, dir_devices, boundary, sea_mask, previous, row_coupling, block_inverse, marks
    )
    return add_step(
        quadrant, cross_gain, quad_coef, sea_mask, wet_tiles,
        previous, row_coupling, block_inverse, entering, halos, halo_entering,
    )


def solution(mesh):
    in_specs = (
        P("dirs", None, "rows", None),
        P("dirs", None, None),
        P("dirs", "rows", None),
        P("dirs"),
        P("dirs", None, None),
        P("dirs"),
        P("rows", None),
        P("rows", None),
        P(),
    )
    out_specs = P("dirs", None, "rows", None)
    return jax.shard_map(
        functools.partial(on_device, mesh.shape["rows"], mesh.shape["dirs"]),
        mesh=mesh, in_specs=in_specs, out_specs=out_specs, check_vma=False,
    )
```
